32 devices in a mesh: dp: 4 (over z), seq: 8 (over y, x, core).
Axes of the slice: x: 2, y: 2, z: 4, core: 2. Of those that a mesh axis runs over, the one named last changes fastest.
Arguments:
- q_video: bfloat16 [12288, 2048], P(('dp', 'seq')), parts along dimension 0, may hold values from -5 to 5
- k_video: bfloat16 [12288, 2048], P(('dp', 'seq')), parts along dimension 0, may hold values from -5 to 5
- v_video: bfloat16 [12288, 2048], P(('dp', 'seq')), parts along dimension 0, may hold values from -6 to 6
- q_audio: bfloat16 [1024, 2048], P(('dp', 'seq')), parts along dimension 0, may hold values from -5 to 5
- k_audio: bfloat16 [1024, 2048], P(('dp', 'seq')), parts along dimension 0, may hold values from -5 to 5
- v_audio: bfloat16 [1024, 2048], P(('dp', 'seq')), parts along dimension 0, may hold values from -6 to 6
Outputs:
- video_out: bfloat16 [12288, 2048], P(('dp', 'seq')), parts along dimension 0
- audio_out: bfloat16 [1024, 2048], P(('dp', 'seq')), parts along dimension 0
The draws below stay inside these ranges and needn't reach their ends.
There are 4 independent parts, one for each index of `dp`. The reference program is written for one: setup_inputs(seed, part) draws one part's arguments, and reference() takes and returns one part's arrays. A program takes and returns all parts, laid end to end along the dimension named above; each array names one. Nothing has to cross between parts.
All inputs are finite; a program needn't handle non-finite values.
Results may differ from the reference program's by a relative error of at most 0.0049.
Values may be sent and summed in bfloat16 or wider, within the bound.
A program may use at most 128 MiB of HBM per device.

```python
import jax
import jax.numpy as jnp
from jax import lax

H = 16
DH = 128
HD = 2048
VIDEO_LEN = 3072
AUDIO_LEN = 256
N_SEQ = 8


def draw_q_video(key, part):
    key = jax.random.fold_in(key, 21)
    return jnp.clip(jax.random.normal(key, (VIDEO_LEN, H * DH), jnp.float32), -5.0, 5.0).astype(jnp.bfloat16)


def draw_k_video(key, part):
    key = jax.random.fold_in(key, 22)
    return jnp.clip(jax.random.normal(key, (VIDEO_LEN, H * DH), jnp.float32), -5.0, 5.0).astype(jnp.bfloat16)


def draw_q_audio(key, part):
    key = jax.random.fold_in(key, 23)
    return jnp.clip(jax.random.normal(key, (AUDIO_LEN, H * DH), jnp.float32), -5.0, 5.0).astype(jnp.bfloat16)


def draw_k_audio(key, part):
    key = jax.random.fold_in(key, 24)
    return jnp.clip(jax.random.normal(key, (AUDIO_LEN, H * DH), jnp.float32), -5.0, 5.0).astype(jnp.bfloat16)


def shard_levels(stream_key, shape, pieces, low, high):
    gain, own = 1.0, jax.random.fold_in(stream_key, 6)
    for position, shards_of in pieces:
        draws = jnp.exp(jax.random.uniform(jax.random.fold_in(own, position), (shards_of,), jnp.float32, low / len(pieces), high / len(pieces)))
        gain = gain * jnp.repeat(draws, shape[position] // shards_of).reshape([-1 if axis == position else 1 for axis in range(len(shape))])
    return gain


def noise(rng, shape, scale, bound, pieces=(), kind=jnp.bfloat16):
    result = jax.random.normal(rng, shape, jnp.float32) * scale
    if len(pieces) > 0:
        result = shard_levels(rng, shape, pieces, -0.22, 0.18) * result
    return jnp.clip(result, min=-bound, max=bound).astype(kind)


def setup_inputs(seed: int = 0, part: int = 0) -> dict:
    seeds = jax.random.split(jax.random.key(seed), 7)
    part_splits = jax.random.split(jax.random.fold_in(seeds[6], part), 7)
    return {
        "q_video": draw_q_video(jax.random.fold_in(jax.random.fold_in(seeds[6], part), 71), part),
        "k_video": draw_k_video(jax.random.fold_in(jax.random.fold_in(seeds[6], part), 71), part),
        "v_video": noise(part_splits[2], (VIDEO_LEN, HD), 1.0, 6.0, ((0, 8),)),
        "q_audio": draw_q_audio(jax.random.fold_in(jax.random.fold_in(seeds[6], part), 71), part),
        "k_audio": draw_k_audio(jax.random.fold_in(jax.random.fold_in(seeds[6], part), 71), part),
        "v_audio": noise(part_splits[5], (AUDIO_LEN, HD), 1.0, 6.0, ((0, 8),)),
    }


def head_major(matrix, head_count):
    return matrix.reshape(matrix.shape[0], head_count, -1).transpose(1, 0, 2)

def settle(mixed):
    return mixed * lax.rsqrt(lax.optimization_barrier(jnp.mean(mixed * mixed, axis=-1, keepdims=True)) + 1e-06)

def video_head(triple):
    queries, key_rows, value_rows = triple
    factor = queries.shape[-1] ** (-0.5)
    scores = jnp.dot(queries, key_rows.T, preferred_element_type=jnp.float32) * factor
    row_peak = lax.optimization_barrier(jnp.max(scores, axis=-1, keepdims=True))
    exponent = jnp.exp(scores - row_peak)
    weights = (exponent / lax.optimization_barrier(jnp.sum(exponent, axis=-1, keepdims=True))).astype(jnp.bfloat16)
    return settle(jnp.dot(weights, value_rows, preferred_element_type=jnp.float32))

def audio_head(triple):
    queries, key_rows, value_rows = triple
    factor = queries.shape[-1] ** (-0.5)
    block_rows = key_rows.shape[0] // N_SEQ
    scores = jnp.dot(queries, key_rows.T, preferred_element_type=jnp.float32) * factor
    scores = scores.reshape(queries.shape[0], N_SEQ, block_rows)
    block_peak = lax.optimization_barrier(jnp.max(scores, axis=-1))
    exponent = jnp.exp(scores - block_peak[..., None])
    totals = lax.optimization_barrier(jnp.sum(exponent, axis=-1))
    rounded = lax.optimization_barrier(exponent.astype(jnp.bfloat16)).astype(jnp.float32)
    blocked_values = value_rows.reshape(N_SEQ, block_rows, -1).astype(jnp.float32)
    numerators = jnp.einsum('asv,svd->asd', rounded, blocked_values)
    overall = lax.optimization_barrier(jnp.max(block_peak, axis=-1, keepdims=True))
    weight = jnp.exp(block_peak - overall)
    summed = lax.optimization_barrier(jnp.sum(numerators * weight[..., None], axis=1))
    denominator = lax.optimization_barrier(jnp.sum(totals * weight, axis=1))
    return settle(summed / denominator[:, None])

def reference(q_video, k_video, v_video, q_audio, k_audio, v_audio):
    video_rows = lax.map(video_head, (head_major(q_video, H), head_major(k_audio, H), head_major(v_audio, H)))
    video_out = video_rows.transpose(1, 0, 2).reshape(q_video.shape[0], -1).astype(jnp.bfloat16)
    audio_rows = lax.map(audio_head, (head_major(q_audio, H), head_major(k_video, H), head_major(v_video, H)))
    audio_out = audio_rows.transpose(1, 0, 2).reshape(q_audio.shape[0], -1).astype(jnp.bfloat16)
    return (video_out, audio_out)
```

```python
import functools

import jax
import jax.numpy as jnp
from jax import lax
from jax.experimental import pallas as pl
from jax.experimental.pallas import tpu as pltpu
from jax.sharding import PartitionSpec as P

H = 16
EPS = 1e-06
LOG2E = 1.4426950408889634
BF16 = jnp.bfloat16
F32 = jnp.float32


def head_major(matrix, head_count):
    return matrix.reshape(matrix.shape[0], head_count, -1).transpose(1, 0, 2)


def settle(mixed):
    return mixed * lax.rsqrt(jnp.mean(mixed * mixed, axis=-1, keepdims=True) + EPS)


def video_head(triple):
    queries, key_rows, value_rows = triple
    factor = queries.shape[-1] ** (-0.5)
    scores = jnp.dot(queries, key_rows.T, preferred_element_type=F32) * factor
    row_peak = jnp.max(scores, axis=-1, keepdims=True)
    exponent = jnp.exp(scores - row_peak)
    weights = (exponent / jnp.sum(exponent, axis=-1, keepdims=True)).astype(BF16)
    return settle(jnp.dot(weights, value_rows, preferred_element_type=F32))


def audio_partial(triple):
    queries, key_rows, value_rows = triple
    factor = queries.shape[-1] ** (-0.5)
    scores = jnp.dot(queries, key_rows.T, preferred_element_type=F32) * factor
    block_peak = jnp.max(scores, axis=-1)
    exponent = jnp.exp(scores - block_peak[:, None])
    totals = jnp.sum(exponent, axis=-1)
    numerators = jnp.dot(exponent.astype(BF16), value_rows, preferred_element_type=F32)
    return (numerators, block_peak, totals)


def local_any(q_video, k_video, v_video, q_audio, k_audio, v_audio):
    all_queries, all_keys, all_values = (
        lax.all_gather(q_audio, "seq", axis=0, tiled=True),
        lax.all_gather(k_audio, "seq", axis=0, tiled=True),
        lax.all_gather(v_audio, "seq", axis=0, tiled=True),
    )
    video_rows = lax.map(
        video_head, (head_major(q_video, H), head_major(all_keys, H), head_major(all_values, H))
    )
    video_out = video_rows.transpose(1, 0, 2).reshape(q_video.shape[0], -1).astype(BF16)
    numerators, block_peak, totals = lax.map(
        audio_partial, (head_major(all_queries, H), head_major(k_video, H), head_major(v_video, H))
    )
    overall = lax.pmax(block_peak.astype(BF16), "seq").astype(block_peak.dtype)
    weight = jnp.exp(block_peak - overall)
    summed, denominator = (
        lax.psum_scatter(numerators * weight[..., None], "seq", scatter_dimension=1, tiled=True),
        lax.psum_scatter(totals * weight, "seq", scatter_dimension=1, tiled=True),
    )
    audio_mix = settle(summed / denominator[..., None])
    audio_out = audio_mix.transpose(1, 0, 2).reshape(audio_mix.shape[1], -1).astype(BF16)
    return (video_out, audio_out)


NT = (((1,), (1,)), ((), ()))


def attend(q, k, v, factor):
    s = lax.dot_general(q, k, NT, preferred_element_type=F32)
    m = jnp.max(s, axis=-1, keepdims=True)
    p = jnp.exp2((s - m) * factor).astype(BF16)
    ve = jnp.concatenate([v, jnp.ones_like(v)], axis=1)
    nd = jnp.dot(p, ve, preferred_element_type=F32)
    d = v.shape[1]
    return m * factor, nd[:, :d], nd[:, d:]


def kernel(
    heads,
    qv, kv, vv, qa, ka, va, vout, aout,
    q_all, k_all, v_all, qv_s, kv_s, vv_s, o_s, ao_s,
    nkeep, nsend, nrecv, msend, mrecv, l_own, l_recv, l_send, l_in,
    g_send, g_recv, p_send, p_recv, r_send, r_recv, loc,
):
    rows = qa.shape[0]
    width = qa.shape[1]
    dh = width // heads
    hw = width // 2
    hh = heads // 2
    keep = 4 * rows
    factor = dh ** (-0.5) * LOG2E

    me = lax.axis_index("seq")
    y, x, c = me // 4, (me // 2) % 2, me % 2

    def dev(yy, xx, cc):
        return {"seq": yy * 4 + xx * 2 + cc}

    X, Y, D, C = dev(y, 1 - x, c), dev(1 - y, x, c), dev(1 - y, 1 - x, c), dev(y, x, 1 - c)
    peers = (None, X, Y, D)

    barrier = pltpu.get_barrier_semaphore()
    for d in (X, Y, D, C):
        pl.semaphore_signal(barrier, inc=1, device_id=d, device_id_type=pl.DeviceIdType.MESH)

    locals_ = []

    def local_copy(src, dst):
        cp = pltpu.make_async_copy(src, dst, loc.at[len(locals_)])
        cp.start()
        locals_.append(cp)
        return cp

    ins = (qa, ka, va)
    alls = (q_all, k_all, v_all)
    c_own = [local_copy(a, b.at[pl.ds(0, rows)]) for a, b in zip(ins, alls)]
    c_kv = local_copy(kv, kv_s)
    c_vv = local_copy(vv, vv_s)
    c_qv = local_copy(qv, qv_s)

    l_own[...] = jnp.zeros_like(l_own)

    units = ((0, 0, 0), (0, 1, 1), (1, 0, 0), (2, 0, 1), (1, 1, 0), (2, 1, 1))

    def g(u, src_slot, dst_slot, to):
        a, h, _ = units[u]
        cols = pl.ds(h * hw, hw)
        if src_slot == 0:
            src = ins[a].at[:, cols]
        else:
            src = alls[a].at[pl.ds(src_slot * rows, rows), cols]
        return pltpu.make_async_remote_copy(
            src_ref=src,
            dst_ref=alls[a].at[pl.ds(dst_slot * rows, rows), cols],
            send_sem=g_send.at[u, dst_slot],
            recv_sem=g_recv.at[u, dst_slot],
            device_id=to,
            device_id_type=pl.DeviceIdType.MESH,
        )

    sent = {}
    started = []

    def go(u, src_slot, dst_slot, to):
        cp = g(u, src_slot, dst_slot, to)
        cp.start()
        sent[u, dst_slot] = cp
        started.append(cp)

    def own(u):
        go(u, 0, 1, X)
        go(u, 0, 2, Y)
        go(u, 0, 4, C)

    def forward_near(u):
        route = units[u][2]
        sent[u, 1].wait_recv()
        if route == 0:
            go(u, 1, 3, Y)
        go(u, 1, 5, C)
        sent[u, 2].wait_recv()
        if route == 1:
            go(u, 2, 3, X)
        go(u, 2, 6, C)

    def forward_far(u):
        sent[u, 3].wait_recv()
        go(u, 3, 7, C)

    def arrived(u):
        for s in (4, 5, 6, 7):
            sent[u, s].wait_recv()

    pl.semaphore_wait(barrier, 4)
    for u in range(6):
        own(u)
    forward_near(0)
    forward_near(1)
    forward_far(0)
    forward_far(1)
    c_own[0].wait()
    c_kv.wait()
    c_vv.wait()
    arrived(0)
    arrived(1)

    def lanes(h):
        return pl.ds(pl.multiple_of(h * dh, dh), dh)

    lane = lax.broadcasted_iota(jnp.int32, (2 * keep, dh), 1)

    def audio(half):
        def body(i, carry):
            for j in range(2):
                i2 = 2 * i + j
                at = lanes(half * hh + i2)
                m, n, d = attend(q_all[:, at], kv_s[:, at], vv_s[:, at], factor)
                n = n * (1.0 / d)
                l_own[half] = jnp.where(lane == i2, m + jnp.log2(d), l_own[half])
                nkeep[:, at] = n[:keep]
                nsend[:, at] = n[keep:].astype(BF16)
            return carry

        lax.fori_loop(0, hh // 2, body, 0)

    def exchange(half):
        cols = pl.ds(half * hw, hw)
        cps = []
        for i, (s, d) in enumerate((
            (nsend.at[:, cols], nrecv.at[:, cols]),
            (l_own.at[half, pl.ds(keep, keep)], l_recv.at[half]),
        )):
            cp = pltpu.make_async_remote_copy(
                src_ref=s, dst_ref=d, send_sem=p_send.at[half, i], recv_sem=p_recv.at[half, i],
                device_id=C, device_id_type=pl.DeviceIdType.MESH,
            )
            cp.start()
            started.append(cp)
            cps.append(cp)
        return cps

    def col(w, h, n):
        sel = lax.broadcasted_iota(jnp.int32, (n, dh), 1) == h
        return jnp.sum(jnp.where(sel, w, 0.0), axis=-1, keepdims=True)

    def merge(half, cps):
        for cp in cps:
            cp.wait_recv()
        l1, l2 = l_own[half, :keep], l_recv[half]
        top = jnp.maximum(l1, l2)
        a1, a2 = jnp.exp2(l1 - top), jnp.exp2(l2 - top)
        tot = a1 + a2
        inv = 1.0 / tot
        w1, w2 = a1 * inv, a2 * inv
        l_send[half] = top + jnp.log2(tot)
        for i in range(hh):
            at = pl.ds((half * hh + i) * dh, dh)
            n = nkeep[:, at] * w1[:, i : i + 1] + nrecv[:, at].astype(F32) * w2[:, i : i + 1]
            msend[:, at] = n.astype(BF16)
        cols = pl.ds(half * hw, hw)
        out = []
        for s in (3, 1, 2):
            r = pl.ds(s * rows, rows)
            for i, (src, dst) in enumerate((
                (msend.at[r, cols], mrecv.at[r, cols]),
                (l_send.at[half, r], l_in.at[half, r]),
            )):
                cp = pltpu.make_async_remote_copy(
                    src_ref=src, dst_ref=dst,
                    send_sem=r_send.at[half, s, i], recv_sem=r_recv.at[half, s, i],
                    device_id=peers[s], device_id_type=pl.DeviceIdType.MESH,
                )
                cp.start()
                started.append(cp)
                out.append(cp)
        return out

    def finish(half, cps):
        for cp in cps:
            cp.wait_recv()
        ls = [l_send[half, :rows]] + [l_in[half, s * rows : (s + 1) * rows] for s in (1, 2, 3)]
        top = functools.reduce(jnp.maximum, ls)
        es = [jnp.exp2(l - top) for l in ls]
        inv = 1.0 / functools.reduce(jnp.add, es)
        ws = [e * inv for e in es]
        for i in range(hh):
            at = pl.ds((half * hh + i) * dh, dh)
            n = msend[:rows, at].astype(F32) * ws[0][:, i : i + 1]
            for s in (1, 2, 3):
                n = n + mrecv[s * rows : (s + 1) * rows, at].astype(F32) * ws[s][:, i : i + 1]
            ao_s[:, at] = settle(n).astype(BF16)

    def video(half):
        def body(i, carry):
            for j in range(2):
                at = lanes(half * hh + 2 * i + j)
                _, n, d = attend(qv_s[:, at], k_all[:, at], v_all[:, at], factor)
                r = lax.rsqrt(jnp.mean(n * n, axis=-1, keepdims=True) + EPS * (d * d))
                o_s[:, at] = (n * r).astype(BF16)
            return carry

        lax.fori_loop(0, hh // 2, body, 0)
        cols = pl.ds(half * hw, hw)
        return local_copy(o_s.at[:, cols], vout.at[:, cols])

    audio(0)
    e0 = exchange(0)
    forward_near(2)
    forward_near(3)
    audio(1)
    e1 = exchange(1)
    forward_far(2)
    forward_far(3)
    m0 = merge(0, e0)
    m1 = merge(1, e1)
    forward_near(4)
    forward_near(5)
    c_own[1].wait()
    c_own[2].wait()
    c_qv.wait()
    arrived(2)
    arrived(3)
    v0 = video(0)
    forward_far(4)
    forward_far(5)
    arrived(4)
    arrived(5)
    v1 = video(1)
    finish(0, m0)
    finish(1, m1)
    ao = local_copy(ao_s, aout)
    for cp in (v0, v1, ao):
        cp.wait()
    for cp in started:
        cp.wait_send()


def local_one(q_video, k_video, v_video, q_audio, k_audio, v_audio):
    vr, width = q_video.shape
    rows = q_audio.shape[0]
    dh = width // H
    keep = 4 * rows
    any_ = pl.BlockSpec(memory_space=pl.ANY)
    dma = pltpu.SemaphoreType.DMA
    return pl.pallas_call(
        functools.partial(kernel, H),
        out_shape=(
            jax.ShapeDtypeStruct((vr, width), BF16),
            jax.ShapeDtypeStruct((rows, width), BF16),
        ),
        in_specs=[any_] * 6,
        out_specs=(any_, any_),
        scratch_shapes=[
            pltpu.VMEM((8 * rows, width), BF16),
            pltpu.VMEM((8 * rows, width), BF16),
            pltpu.VMEM((8 * rows, width), BF16),
            pltpu.VMEM((vr, width), BF16),
            pltpu.VMEM((vr, width), BF16),
            pltpu.VMEM((vr, width), BF16),
            pltpu.VMEM((vr, width), BF16),
            pltpu.VMEM((rows, width), BF16),
            pltpu.VMEM((keep, width), F32),
            pltpu.VMEM((keep, width), BF16),
            pltpu.VMEM((keep, width), BF16),
            pltpu.VMEM((keep, width), BF16),
            pltpu.VMEM((keep, width), BF16),
            pltpu.VMEM((2, 2 * keep, dh), F32),
            pltpu.VMEM((2, keep, dh), F32),
            pltpu.VMEM((2, keep, dh), F32),
            pltpu.VMEM((2, keep, dh), F32),
            dma((6, 8)),
            dma((6, 8)),
            dma((2, 2)),
            dma((2, 2)),
            dma((2, 4, 2)),
            dma((2, 4, 2)),
            dma((9,)),
        ],
        compiler_params=pltpu.CompilerParams(
            collective_id=0, has_side_effects=True, vmem_limit_bytes=48 * 1024 * 1024
        ),
    )(q_video, k_video, v_video, q_audio, k_audio, v_audio)


def solution(mesh):
    spec = P(("dp", "seq"), None)
    return jax.shard_map(
        local_one if mesh.shape["seq"] == 8 else local_any,
        mesh=mesh,
        in_specs=(spec,) * 6,
        out_specs=(spec, spec),
        check_vma=False,
    )
```

```python
import functools

import jax
import jax.numpy as jnp
from jax import lax
from jax.experimental import pallas as pl
from jax.experimental.pallas import tpu as pltpu
from jax.sharding import PartitionSpec as P

H = 16
EPS = 1e-06
LOG2E = 1.4426950408889634
BF16 = jnp.bfloat16
F32 = jnp.float32


def head_major(matrix, head_count):
    return matrix.reshape(matrix.shape[0], head_count, -1).transpose(1, 0, 2)


def settle(mixed):
    return mixed * lax.rsqrt(jnp.mean(mixed * mixed, axis=-1, keepdims=True) + EPS)


def video_head(triple):
    queries, key_rows, value_rows = triple
    factor = queries.shape[-1] ** (-0.5)
    scores = jnp.dot(queries, key_rows.T, preferred_element_type=F32) * factor
    row_peak = jnp.max(scores, axis=-1, keepdims=True)
    exponent = jnp.exp(scores - row_peak)
    weights = (exponent / jnp.sum(exponent, axis=-1, keepdims=True)).astype(BF16)
    return settle(jnp.dot(weights, value_rows, preferred_element_type=F32))


def audio_partial(triple):
    queries, key_rows, value_rows = triple
    factor = queries.shape[-1] ** (-0.5)
    scores = jnp.dot(queries, key_rows.T, preferred_element_type=F32) * factor
    block_peak = jnp.max(scores, axis=-1)
    exponent = jnp.exp(scores - block_peak[:, None])
    totals = jnp.sum(exponent, axis=-1)
    numerators = jnp.dot(exponent.astype(BF16), value_rows, preferred_element_type=F32)
    return (numerators, block_peak, totals)


def local_any(q_video, k_video, v_video, q_audio, k_audio, v_audio):
    all_queries, all_keys, all_values = (
        lax.all_gather(q_audio, "seq", axis=0, tiled=True),
        lax.all_gather(k_audio, "seq", axis=0, tiled=True),
        lax.all_gather(v_audio, "seq", axis=0, tiled=True),
    )
    video_rows = lax.map(
        video_head, (head_major(q_video, H), head_major(all_keys, H), head_major(all_values, H))
    )
    video_out = video_rows.transpose(1, 0, 2).reshape(q_video.shape[0], -1).astype(BF16)
    numerators, block_peak, totals = lax.map(
        audio_partial, (head_major(all_queries, H), head_major(k_video, H), head_major(v_video, H))
    )
    overall = lax.pmax(block_peak.astype(BF16), "seq").astype(block_peak.dtype)
    weight = jnp.exp(block_peak - overall)
    summed, denominator = (
        lax.psum_scatter(numerators * weight[..., None], "seq", scatter_dimension=1, tiled=True),
        lax.psum_scatter(totals * weight, "seq", scatter_dimension=1, tiled=True),
    )
    audio_mix = settle(summed / denominator[..., None])
    audio_out = audio_mix.transpose(1, 0, 2).reshape(audio_mix.shape[1], -1).astype(BF16)
    return (video_out, audio_out)


NT = (((1,), (1,)), ((), ()))
TN = (((0,), (0,)), ((), ()))


def attend(q, k, v, factor):
    s = lax.dot_general(k, q, NT, preferred_element_type=F32)
    m = jnp.max(s, axis=0, keepdims=True)
    e = jnp.exp2((s - m) * factor)
    n = lax.dot_general(e.astype(BF16), v, TN, preferred_element_type=F32)
    return m * factor, n, jnp.sum(e, axis=0, keepdims=True)


def kernel(
    heads,
    qv, kv, vv, qa, ka, va, vout, aout,
    q_all, k_all, v_all, qv_s, kv_s, vv_s, o_s, ao_s,
    nkeep, nsend, nrecv, msend, mrecv, l_own, l_recv, l_send, l_in,
    g_send, g_recv, p_send, p_recv, r_send, r_recv, loc,
):
    rows = qa.shape[0]
    width = qa.shape[1]
    dh = width // heads
    hw = width // 2
    hh = heads // 2
    keep = 4 * rows
    factor = dh ** (-0.5) * LOG2E

    me = lax.axis_index("seq")
    y, x, c = me // 4, (me // 2) % 2, me % 2

    def dev(yy, xx, cc):
        return {"seq": yy * 4 + xx * 2 + cc}

    X, Y, D, C = dev(y, 1 - x, c), dev(1 - y, x, c), dev(1 - y, 1 - x, c), dev(y, x, 1 - c)
    peers = (None, X, Y, D)

    barrier = pltpu.get_barrier_semaphore()
    for d in (X, Y, D, C):
        pl.semaphore_signal(barrier, inc=1, device_id=d, device_id_type=pl.DeviceIdType.MESH)

    locals_ = []

    def local_copy(src, dst):
        cp = pltpu.make_async_copy(src, dst, loc.at[len(locals_)])
        cp.start()
        locals_.append(cp)
        return cp

    ins = (qa, ka, va)
    alls = (q_all, k_all, v_all)
    c_own = [local_copy(a, b.at[pl.ds(0, rows)]) for a, b in zip(ins, alls)]
    c_kv = local_copy(kv, kv_s)
    c_vv = local_copy(vv, vv_s)
    c_qv = local_copy(qv, qv_s)

    units = ((0, 0, 0), (0, 1, 1), (1, 0, 0), (2, 0, 1), (1, 1, 0), (2, 1, 1))

    def g(u, src_slot, dst_slot, to):
        a, h, _ = units[u]
        cols = pl.ds(h * hw, hw)
        if src_slot == 0:
            src = ins[a].at[:, cols]
        else:
            src = alls[a].at[pl.ds(src_slot * rows, rows), cols]
        return pltpu.make_async_remote_copy(
            src_ref=src,
            dst_ref=alls[a].at[pl.ds(dst_slot * rows, rows), cols],
            send_sem=g_send.at[u, dst_slot],
            recv_sem=g_recv.at[u, dst_slot],
            device_id=to,
            device_id_type=pl.DeviceIdType.MESH,
        )

    sent = {}
    started = []

    def go(u, src_slot, dst_slot, to):
        cp = g(u, src_slot, dst_slot, to)
        cp.start()
        sent[u, dst_slot] = cp
        started.append(cp)

    def own(u):
        go(u, 0, 1, X)
        go(u, 0, 2, Y)
        go(u, 0, 4, C)
        if u in (0, 1, 2, 3):
            go(u, 0, 3, D)

    def forward_near(u):
        route = units[u][2]
        sent[u, 1].wait_recv()
        if route == 0 and u not in (0, 1, 2, 3):
            go(u, 1, 3, Y)
        go(u, 1, 5, C)
        sent[u, 2].wait_recv()
        if route == 1 and u not in (0, 1, 2, 3):
            go(u, 2, 3, X)
        go(u, 2, 6, C)

    def forward_far(u):
        sent[u, 3].wait_recv()
        go(u, 3, 7, C)

    def arrived(u):
        for s in (4, 5, 6, 7):
            sent[u, s].wait_recv()

    def lanes(h):
        return pl.ds(pl.multiple_of(h * dh, dh), dh)

    def audio(first, last):
        half = first // hh

        def body(i, carry):
            for j in range(4):
                i2 = 4 * i + j - half * hh
                at = lanes(4 * i + j)
                m, n, d = attend(q_all[:, at], kv_s[:, at], vv_s[:, at], factor)
                n = n * (1.0 / d).T
                l_own[half, pl.ds(i2, 1)] = m + jnp.log2(d)
                nkeep[:, at] = n[:keep]
                nsend[:, at] = n[keep:].astype(BF16)
            return carry

        lax.fori_loop(first // 4, last // 4, body, 0)

    def exchange(half):
        cols = pl.ds(half * hw, hw)
        cps = []
        for i, (s, d) in enumerate((
            (nsend.at[:, cols], nrecv.at[:, cols]),
            (l_own.at[half, :, pl.ds(keep, keep)], l_recv.at[half]),
        )):
            cp = pltpu.make_async_remote_copy(
                src_ref=s, dst_ref=d, send_sem=p_send.at[half, i], recv_sem=p_recv.at[half, i],
                device_id=C, device_id_type=pl.DeviceIdType.MESH,
            )
            cp.start()
            started.append(cp)
            cps.append(cp)
        return cps

    def merge(half, cps):
        for cp in cps:
            cp.wait_recv()
        l1, l2 = l_own[half, :, :keep], l_recv[half]
        top = jnp.maximum(l1, l2)
        a1, a2 = jnp.exp2(l1 - top), jnp.exp2(l2 - top)
        tot = a1 + a2
        inv = 1.0 / tot
        w1, w2 = (a1 * inv).T, (a2 * inv).T
        l_send[half] = top + jnp.log2(tot)
        for i in range(hh):
            at = pl.ds((half * hh + i) * dh, dh)
            n = nkeep[:, at] * w1[:, i : i + 1] + nrecv[:, at].astype(F32) * w2[:, i : i + 1]
            msend[:, at] = n.astype(BF16)
        cols = pl.ds(half * hw, hw)
        out = []
        for s in (3, 1, 2):
            r = pl.ds(s * rows, rows)
            for i, (src, dst) in enumerate((
                (msend.at[r, cols], mrecv.at[r, cols]),
                (l_send.at[half], l_in.at[half, s]),
            )):
                cp = pltpu.make_async_remote_copy(
                    src_ref=src, dst_ref=dst,
                    send_sem=r_send.at[half, s, i], recv_sem=r_recv.at[half, s, i],
                    device_id=peers[s], device_id_type=pl.DeviceIdType.MESH,
                )
                cp.start()
                started.append(cp)
                out.append(cp)
        return out

    def finish(half, cps):
        for cp in cps:
            cp.wait_recv()
        ls = [l_send[half].T[:rows]] + [l_in[half, s].T[s * rows : (s + 1) * rows] for s in (1, 2, 3)]
        top = functools.reduce(jnp.maximum, ls)
        es = [jnp.exp2(l - top) for l in ls]
        inv = 1.0 / functools.reduce(jnp.add, es)
        ws = [e * inv for e in es]
        for i in range(hh):
            at = pl.ds((half * hh + i) * dh, dh)
            n = msend[:rows, at].astype(F32) * ws[0][:, i : i + 1]
            for s in (1, 2, 3):
                n = n + mrecv[s * rows : (s + 1) * rows, at].astype(F32) * ws[s][:, i : i + 1]
            ao_s[:, at] = settle(n).astype(BF16)

    def video(first, last):
        def body(i, carry):
            for j in range(4):
                at = lanes(4 * i + j)
                _, n, d = attend(qv_s[:, at], k_all[:, at], v_all[:, at], factor)
                r = lax.rsqrt(jnp.mean(n * n, axis=-1, keepdims=True) + (EPS * (d * d)).T)
                o_s[:, at] = (n * r).astype(BF16)
            return carry

        lax.fori_loop(first // 4, last // 4, body, 0)
        cols = pl.ds(first * dh, (last - first) * dh)
        return local_copy(o_s.at[:, cols], vout.at[:, cols])

    q4 = hh // 2
    pl.semaphore_wait(barrier, 4)
    own(0)
    own(1)
    forward_near(0)
    forward_near(1)
    own(2)
    own(3)
    forward_far(0)
    forward_far(1)
    c_own[0].wait()
    c_kv.wait()
    c_vv.wait()
    arrived(0)
    arrived(1)
    audio(0, hh)
    e0 = exchange(0)
    own(4)
    own(5)
    forward_near(2)
    forward_near(3)
    audio(hh, heads)
    e1 = exchange(1)
    forward_far(2)
    forward_far(3)
    m0 = merge(0, e0)
    forward_near(4)
    forward_near(5)
    m1 = merge(1, e1)
    c_own[1].wait()
    c_own[2].wait()
    c_qv.wait()
    arrived(2)
    arrived(3)
    v0 = video(0, hh)
    forward_far(4)
    forward_far(5)
    finish(0, m0)
    arrived(4)
    arrived(5)
    v1 = video(hh, heads)
    finish(1, m1)
    ao = local_copy(ao_s, aout)
    for cp in (v0, v1, ao):
        cp.wait()
    for cp in started:
        cp.wait_send()


def land_kernel(v, a, vout, aout, vbuf, abuf, s_in, s_out, *, pieces):
    step = v.shape[0] // pieces
    pairs = [(a, abuf, aout)]
    for i in range(pieces):
        r = pl.ds(i * step, step)
        pairs.append((v.at[r], vbuf.at[r], vout.at[r]))
    ins = [pltpu.make_async_copy(p[0], p[1], s_in.at[i]) for i, p in enumerate(pairs)]
    outs = [pltpu.make_async_copy(p[1], p[2], s_out.at[i]) for i, p in enumerate(pairs)]
    for cp in ins:
        cp.start()
    for i, cp in enumerate(ins):
        cp.wait()
        outs[i].start()
    for cp in outs:
        cp.wait()


def land(v, a, pieces=6):
    any_ = pl.BlockSpec(memory_space=pl.ANY)
    return pl.pallas_call(
        functools.partial(land_kernel, pieces=pieces),
        out_shape=(jax.ShapeDtypeStruct(v.shape, v.dtype), jax.ShapeDtypeStruct(a.shape, a.dtype)),
        in_specs=[any_] * 2,
        out_specs=(any_, any_),
        scratch_shapes=[
            pltpu.VMEM(v.shape, v.dtype),
            pltpu.VMEM(a.shape, a.dtype),
            pltpu.SemaphoreType.DMA((pieces + 1,)),
            pltpu.SemaphoreType.DMA((pieces + 1,)),
        ],
        compiler_params=pltpu.CompilerParams(vmem_limit_bytes=63 * 1024 * 1024),
    )(v, a)


def local_one(q_video, k_video, v_video, q_audio, k_audio, v_audio):
    vr, width = q_video.shape
    rows = q_audio.shape[0]
    dh = width // H
    keep = 4 * rows
    any_ = pl.BlockSpec(memory_space=pl.ANY)
    dma = pltpu.SemaphoreType.DMA
    return land(*pl.pallas_call(
        functools.partial(kernel, H),
        out_shape=(
            jax.ShapeDtypeStruct((vr, width), BF16),
            jax.ShapeDtypeStruct((rows, width), BF16),
        ),
        in_specs=[any_] * 6,
        out_specs=(any_, any_),
        scratch_shapes=[
            pltpu.VMEM((8 * rows, width), BF16),
            pltpu.VMEM((8 * rows, width), BF16),
            pltpu.VMEM((8 * rows, width), BF16),
            pltpu.VMEM((vr, width), BF16),
            pltpu.VMEM((vr, width), BF16),
            pltpu.VMEM((vr, width), BF16),
            pltpu.VMEM((vr, width), BF16),
            pltpu.VMEM((rows, width), BF16),
            pltpu.VMEM((keep, width), F32),
            pltpu.VMEM((keep, width), BF16),
            pltpu.VMEM((keep, width), BF16),
            pltpu.VMEM((keep, width), BF16),
            pltpu.VMEM((keep, width), BF16),
            pltpu.VMEM((2, H // 2, 2 * keep), F32),
            pltpu.VMEM((2, H // 2, keep), F32),
            pltpu.VMEM((2, H // 2, keep), F32),
            pltpu.VMEM((2, 4, H // 2, keep), F32),
            dma((6, 8)),
            dma((6, 8)),
            dma((2, 2)),
            dma((2, 2)),
            dma((2, 4, 2)),
            dma((2, 4, 2)),
            dma((11,)),
        ],
        compiler_params=pltpu.CompilerParams(
            collective_id=0, has_side_effects=True, vmem_limit_bytes=63 * 1024 * 1024
        ),
    )(q_video, k_video, v_video, q_audio, k_audio, v_audio))


def solution(mesh):
    spec = P(("dp", "seq"), None)
    return jax.shard_map(
        local_one if mesh.shape["seq"] == 8 else local_any,
        mesh=mesh,
        in_specs=(spec,) * 6,
        out_specs=(spec, spec),
        check_vma=False,
    )
```

```python
import functools

import jax
import jax.numpy as jnp
from jax import lax
from jax.experimental import pallas as pl
from jax.experimental.pallas import tpu as pltpu
from jax.sharding import PartitionSpec as P

H = 16
EPS = 1e-06
LOG2E = 1.4426950408889634
BF16 = jnp.bfloat16
F32 = jnp.float32


def head_major(matrix, head_count):
    return matrix.reshape(matrix.shape[0], head_count, -1).transpose(1, 0, 2)


def settle(mixed):
    return mixed * lax.rsqrt(jnp.mean(mixed * mixed, axis=-1, keepdims=True) + EPS)


def video_head(triple):
    queries, key_rows, value_rows = triple
    factor = queries.shape[-1] ** (-0.5)
    scores = jnp.dot(queries, key_rows.T, preferred_element_type=F32) * factor
    row_peak = jnp.max(scores, axis=-1, keepdims=True)
    exponent = jnp.exp(scores - row_peak)
    weights = (exponent / jnp.sum(exponent, axis=-1, keepdims=True)).astype(BF16)
    return settle(jnp.dot(weights, value_rows, preferred_element_type=F32))


def audio_partial(triple):
    queries, key_rows, value_rows = triple
    factor = queries.shape[-1] ** (-0.5)
    scores = jnp.dot(queries, key_rows.T, preferred_element_type=F32) * factor
    block_peak = jnp.max(scores, axis=-1)
    exponent = jnp.exp(scores - block_peak[:, None])
    totals = jnp.sum(exponent, axis=-1)
    numerators = jnp.dot(exponent.astype(BF16), value_rows, preferred_element_type=F32)
    return (numerators, block_peak, totals)


def local_any(q_video, k_video, v_video, q_audio, k_audio, v_audio):
    all_queries, all_keys, all_values = (
        lax.all_gather(q_audio, "seq", axis=0, tiled=True),
        lax.all_gather(k_audio, "seq", axis=0, tiled=True),
        lax.all_gather(v_audio, "seq", axis=0, tiled=True),
    )
    video_rows = lax.map(
        video_head, (head_major(q_video, H), head_major(all_keys, H), head_major(all_values, H))
    )
    video_out = video_rows.transpose(1, 0, 2).reshape(q_video.shape[0], -1).astype(BF16)
    numerators, block_peak, totals = lax.map(
        audio_partial, (head_major(all_queries, H), head_major(k_video, H), head_major(v_video, H))
    )
    overall = lax.pmax(block_peak.astype(BF16), "seq").astype(block_peak.dtype)
    weight = jnp.exp(block_peak - overall)
    summed, denominator = (
        lax.psum_scatter(numerators * weight[..., None], "seq", scatter_dimension=1, tiled=True),
        lax.psum_scatter(totals * weight, "seq", scatter_dimension=1, tiled=True),
    )
    audio_mix = settle(summed / denominator[..., None])
    audio_out = audio_mix.transpose(1, 0, 2).reshape(audio_mix.shape[1], -1).astype(BF16)
    return (video_out, audio_out)


NT = (((1,), (1,)), ((), ()))
TN = (((0,), (0,)), ((), ()))


def attend(q, k, v, factor):
    s = lax.dot_general(k, q, NT, preferred_element_type=F32)
    m = jnp.max(s, axis=0, keepdims=True)
    e = jnp.exp2((s - m) * factor)
    n = lax.dot_general(e.astype(BF16), v, TN, preferred_element_type=F32)
    return m * factor, n, jnp.sum(e, axis=0, keepdims=True)


def kernel(
    heads,
    qv, kv, vv, qa, ka, va, vout, aout,
    q_all, k_all, v_all, qv_s, kv_s, vv_s, o_s, ao_s,
    nkeep, nsend, nrecv, msend, mrecv, l_own, l_recv, l_send, l_in,
    g_send, g_recv, p_send, p_recv, r_send, r_recv, loc,
):
    rows = qa.shape[0]
    width = qa.shape[1]
    dh = width // heads
    hw = width // 2
    hh = heads // 2
    keep = 4 * rows
    factor = dh ** (-0.5) * LOG2E

    me = lax.axis_index("seq")
    y, x, c = me // 4, (me // 2) % 2, me % 2

    def dev(yy, xx, cc):
        return {"seq": yy * 4 + xx * 2 + cc}

    X, Y, D, C = dev(y, 1 - x, c), dev(1 - y, x, c), dev(1 - y, 1 - x, c), dev(y, x, 1 - c)
    peers = (None, X, Y, D)

    barrier = pltpu.get_barrier_semaphore()
    for d in (X, Y, D, C):
        pl.semaphore_signal(barrier, inc=1, device_id=d, device_id_type=pl.DeviceIdType.MESH)

    locals_ = []

    def local_copy(src, dst):
        cp = pltpu.make_async_copy(src, dst, loc.at[len(locals_)])
        cp.start()
        locals_.append(cp)
        return cp

    ins = (qa, ka, va)
    alls = (q_all, k_all, v_all)
    c_own = [local_copy(a, b.at[pl.ds(0, rows)]) for a, b in zip(ins, alls)]
    c_kv = local_copy(kv, kv_s)
    c_vv = local_copy(vv, vv_s)
    c_qv = local_copy(qv, qv_s)

    units = ((0, 0, 0), (0, 1, 1), (1, 0, 0), (2, 0, 1), (1, 1, 0), (2, 1, 1))

    def g(u, src_slot, dst_slot, to):
        a, h, _ = units[u]
        cols = pl.ds(h * hw, hw)
        if src_slot == 0:
            src = ins[a].at[:, cols]
        else:
            src = alls[a].at[pl.ds(src_slot * rows, rows), cols]
        return pltpu.make_async_remote_copy(
            src_ref=src,
            dst_ref=alls[a].at[pl.ds(dst_slot * rows, rows), cols],
            send_sem=g_send.at[u, dst_slot],
            recv_sem=g_recv.at[u, dst_slot],
            device_id=to,
            device_id_type=pl.DeviceIdType.MESH,
        )

    sent = {}
    started = []

    def go(u, src_slot, dst_slot, to):
        cp = g(u, src_slot, dst_slot, to)
        cp.start()
        sent[u, dst_slot] = cp
        started.append(cp)

    def own(u):
        go(u, 0, 1, X)
        go(u, 0, 2, Y)
        go(u, 0, 4, C)
        if u in (0, 1, 2, 3):
            go(u, 0, 3, D)

    def forward_near(u):
        route = units[u][2]
        sent[u, 1].wait_recv()
        if route == 0 and u not in (0, 1, 2, 3):
            go(u, 1, 3, Y)
        go(u, 1, 5, C)
        sent[u, 2].wait_recv()
        if route == 1 and u not in (0, 1, 2, 3):
            go(u, 2, 3, X)
        go(u, 2, 6, C)

    def forward_far(u):
        sent[u, 3].wait_recv()
        go(u, 3, 7, C)

    def arrived(u):
        for s in (4, 5, 6, 7):
            sent[u, s].wait_recv()

    def lanes(h):
        return pl.ds(pl.multiple_of(h * dh, dh), dh)

    def audio(first, last):
        half = first // hh

        def body(i, carry):
            for j in range(4):
                i2 = 4 * i + j - half * hh
                at = lanes(4 * i + j)
                m, n, d = attend(q_all[:, at], kv_s[:, at], vv_s[:, at], factor)
                n = n * (1.0 / d).T
                l_own[half, pl.ds(i2, 1)] = m + jnp.log2(d)
                nkeep[:, at] = n[:keep]
                nsend[:, at] = n[keep:].astype(BF16)
            return carry

        lax.fori_loop(first // 4, last // 4, body, 0)

    def exchange(half):
        cols = pl.ds(half * hw, hw)
        cps = []
        for i, (s, d) in enumerate((
            (nsend.at[:, cols], nrecv.at[:, cols]),
            (l_own.at[half, :, pl.ds(keep, keep)], l_recv.at[half]),
        )):
            cp = pltpu.make_async_remote_copy(
                src_ref=s, dst_ref=d, send_sem=p_send.at[half, i], recv_sem=p_recv.at[half, i],
                device_id=C, device_id_type=pl.DeviceIdType.MESH,
            )
            cp.start()
            started.append(cp)
            cps.append(cp)
        return cps

    def merge(half, cps):
        for cp in cps:
            cp.wait_recv()
        l1, l2 = l_own[half, :, :keep], l_recv[half]
        top = jnp.maximum(l1, l2)
        a1, a2 = jnp.exp2(l1 - top), jnp.exp2(l2 - top)
        tot = a1 + a2
        inv = 1.0 / tot
        w1, w2 = (a1 * inv).T, (a2 * inv).T
        l_send[half] = top + jnp.log2(tot)
        for i in range(hh):
            at = pl.ds((half * hh + i) * dh, dh)
            n = nkeep[:, at] * w1[:, i : i + 1] + nrecv[:, at].astype(F32) * w2[:, i : i + 1]
            msend[:, at] = n.astype(BF16)
        cols = pl.ds(half * hw, hw)
        out = []
        for s in (3, 1, 2):
            r = pl.ds(s * rows, rows)
            for i, (src, dst) in enumerate((
                (msend.at[r, cols], mrecv.at[r, cols]),
                (l_send.at[half], l_in.at[half, s]),
            )):
                cp = pltpu.make_async_remote_copy(
                    src_ref=src, dst_ref=dst,
                    send_sem=r_send.at[half, s, i], recv_sem=r_recv.at[half, s, i],
                    device_id=peers[s], device_id_type=pl.DeviceIdType.MESH,
                )
                cp.start()
                started.append(cp)
                out.append(cp)
        return out

    def finish(half, cps):
        for cp in cps:
            cp.wait_recv()
        ls = [l_send[half].T[:rows]] + [l_in[half, s].T[s * rows : (s + 1) * rows] for s in (1, 2, 3)]
        top = functools.reduce(jnp.maximum, ls)
        es = [jnp.exp2(l - top) for l in ls]
        inv = 1.0 / functools.reduce(jnp.add, es)
        ws = [e * inv for e in es]
        for i in range(hh):
            at = pl.ds((half * hh + i) * dh, dh)
            n = msend[:rows, at].astype(F32) * ws[0][:, i : i + 1]
            for s in (1, 2, 3):
                n = n + mrecv[s * rows : (s + 1) * rows, at].astype(F32) * ws[s][:, i : i + 1]
            ao_s[:, at] = settle(n).astype(BF16)

    def video(first, last):
        def body(i, carry):
            for j in range(4):
                at = lanes(4 * i + j)
                _, n, d = attend(qv_s[:, at], k_all[:, at], v_all[:, at], factor)
                r = lax.rsqrt(jnp.mean(n * n, axis=-1, keepdims=True) + (EPS * (d * d)).T)
                o_s[:, at] = (n * r).astype(BF16)
            return carry

        lax.fori_loop(first // 4, last // 4, body, 0)
        cols = pl.ds(first * dh, (last - first) * dh)
        return local_copy(o_s.at[:, cols], vout.at[:, cols])

    q4 = hh // 2
    pl.semaphore_wait(barrier, 4)
    own(0)
    own(1)
    forward_near(0)
    forward_near(1)
    own(2)
    own(3)
    forward_far(0)
    forward_far(1)
    c_own[0].wait()
    c_kv.wait()
    c_vv.wait()
    arrived(0)
    arrived(1)
    audio(0, hh)
    e0 = exchange(0)
    own(4)
    own(5)
    forward_near(2)
    forward_near(3)
    audio(hh, heads)
    e1 = exchange(1)
    forward_far(2)
    forward_far(3)
    m0 = merge(0, e0)
    forward_near(4)
    forward_near(5)
    c_own[1].wait()
    c_own[2].wait()
    c_qv.wait()
    arrived(2)
    arrived(3)
    v0 = video(0, hh)
    m1 = merge(1, e1)
    forward_far(4)
    forward_far(5)
    finish(0, m0)
    arrived(4)
    arrived(5)
    v1 = video(hh, heads)
    finish(1, m1)
    ao = local_copy(ao_s, aout)
    for cp in (v0, v1, ao):
        cp.wait()
    for cp in started:
        cp.wait_send()


def land_kernel(v, a, vout, aout, vbuf, abuf, s_in, s_out, *, pieces):
    step = v.shape[0] // pieces
    pairs = [(a, abuf, aout)]
    for i in range(pieces):
        r = pl.ds(i * step, step)
        pairs.append((v.at[r], vbuf.at[r], vout.at[r]))
    ins = [pltpu.make_async_copy(p[0], p[1], s_in.at[i]) for i, p in enumerate(pairs)]
    outs = [pltpu.make_async_copy(p[1], p[2], s_out.at[i]) for i, p in enumerate(pairs)]
    for cp in ins:
        cp.start()
    for i, cp in enumerate(ins):
        cp.wait()
        outs[i].start()
    for cp in outs:
        cp.wait()


def land(v, a, pieces=6):
    any_ = pl.BlockSpec(memory_space=pl.ANY)
    return pl.pallas_call(
        functools.partial(land_kernel, pieces=pieces),
        out_shape=(jax.ShapeDtypeStruct(v.shape, v.dtype), jax.ShapeDtypeStruct(a.shape, a.dtype)),
        in_specs=[any_] * 2,
        out_specs=(any_, any_),
        scratch_shapes=[
            pltpu.VMEM(v.shape, v.dtype),
            pltpu.VMEM(a.shape, a.dtype),
            pltpu.SemaphoreType.DMA((pieces + 1,)),
            pltpu.SemaphoreType.DMA((pieces + 1,)),
        ],
        compiler_params=pltpu.CompilerParams(vmem_limit_bytes=63 * 1024 * 1024),
    )(v, a)


def local_one(q_video, k_video, v_video, q_audio, k_audio, v_audio):
    vr, width = q_video.shape
    rows = q_audio.shape[0]
    dh = width // H
    keep = 4 * rows
    any_ = pl.BlockSpec(memory_space=pl.ANY)
    dma = pltpu.SemaphoreType.DMA
    return land(*pl.pallas_call(
        functools.partial(kernel, H),
        out_shape=(
            jax.ShapeDtypeStruct((vr, width), BF16),
            jax.ShapeDtypeStruct((rows, width), BF16),
        ),
        in_specs=[any_] * 6,
        out_specs=(any_, any_),
        scratch_shapes=[
            pltpu.VMEM((8 * rows, width), BF16),
            pltpu.VMEM((8 * rows, width), BF16),
            pltpu.VMEM((8 * rows, width), BF16),
            pltpu.VMEM((vr, width), BF16),
            pltpu.VMEM((vr, width), BF16),
            pltpu.VMEM((vr, width), BF16),
            pltpu.VMEM((vr, width), BF16),
            pltpu.VMEM((rows, width), BF16),
            pltpu.VMEM((keep, width), F32),
            pltpu.VMEM((keep, width), BF16),
            pltpu.VMEM((keep, width), BF16),
            pltpu.VMEM((keep, width), BF16),
            pltpu.VMEM((keep, width), BF16),
            pltpu.VMEM((2, H // 2, 2 * keep), F32),
            pltpu.VMEM((2, H // 2, keep), F32),
            pltpu.VMEM((2, H // 2, keep), F32),
            pltpu.VMEM((2, 4, H // 2, keep), F32),
            dma((6, 8)),
            dma((6, 8)),
            dma((2, 2)),
            dma((2, 2)),
            dma((2, 4, 2)),
            dma((2, 4, 2)),
            dma((11,)),
        ],
        compiler_params=pltpu.CompilerParams(
            collective_id=0, has_side_effects=True, vmem_limit_bytes=63 * 1024 * 1024
        ),
    )(q_video, k_video, v_video, q_audio, k_audio, v_audio))


def solution(mesh):
    spec = P(("dp", "seq"), None)
    return jax.shard_map(
        local_one if mesh.shape["seq"] == 8 else local_any,
        mesh=mesh,
        in_specs=(spec,) * 6,
        out_specs=(spec, spec),
        check_vma=False,
    )
```
